32 devices in a mesh: seq: 8 (over z, x), fsdp: 4 (over y, core).
Axes of the slice: x: 2, y: 2, z: 4, core: 2. Of those that a mesh axis runs over, the one named last changes fastest.
Arguments:
- tokens: bfloat16 [4, 8192, 768], P('fsdp', 'seq'), may hold values from -6 to 6
- cotangent: bfloat16 [4, 8192, 768], P('fsdp', 'seq'), may hold values from -6 to 6
- starts: int32 [4, 3], P('fsdp'), may hold values from 0 to 7680, as said below
- w_qkv: bfloat16 [768, 2304], P('fsdp'), may hold values from -0.21875 to 0.21875
- w_attn: bfloat16 [768, 768], P('fsdp'), may hold values from -0.625 to 0.625
- w_in: bfloat16 [768, 2304], P('fsdp'), may hold values from -0.21875 to 0.21875
- w_out: bfloat16 [1152, 768], P('fsdp'), may hold values from -0.1875 to 0.1875
- gain_one: bfloat16 [768], P('fsdp'), may hold values from 0.25 to 1.75
- gain_two: bfloat16 [768], P('fsdp'), may hold values from 0.25 to 1.75
Outputs:
- result: bfloat16 [4, 8192, 768], P('fsdp', 'seq')
- grad_tokens: bfloat16 [4, 8192, 768], P('fsdp', 'seq')
- grad_qkv: float32 [768, 2304], P('fsdp')
- grad_attn: float32 [768, 768], P('fsdp')
- grad_in: float32 [768, 2304], P('fsdp')
- grad_out: float32 [1152, 768], P('fsdp')
- grad_gain_one: float32 [768], P('fsdp')
- grad_gain_two: float32 [768], P('fsdp')
The draws below stay inside these ranges and needn't reach their ends.
Inputs may be any that keep to these rules, and one draw needn't show every extreme that they name: `starts`: row g lists in rising order the first token of each of the 3 sequences of group g: the first is 0 and the last is 7680; the middle one lies either between 256 and 512 or is exactly 7424, so that one sequence of each group reaches from the first token shard to the last.
All inputs are finite; a program needn't handle non-finite values.
Results may differ from the reference program's by a relative error of at most 0.018.
Values may be sent and summed in bfloat16 or wider, within the bound.
A program may use at most 192 MiB of HBM per device.

```python
import math
import jax
import jax.numpy as jnp
from jax import lax

D = 768
HEADS = 12
HD = 64
FF = 1152
HALF = 64
TOK_DEV = 1024
GROUP_TOK = 8192
N_FSDP = 4


def draw_starts(key, part):
    key = jax.random.fold_in(key, 7)
    key_side, key_early, key_late = jax.random.split(key, 3)
    side = jax.random.randint(key_side, (N_FSDP,), 0, 2)
    early = jax.random.randint(key_early, (N_FSDP,), TOK_DEV // 4, TOK_DEV // 2 + 1)
    late = jax.random.randint(key_late, (N_FSDP,), GROUP_TOK - TOK_DEV + TOK_DEV // 4, GROUP_TOK - 3 * TOK_DEV // 4 + 1)
    middle = jnp.where(side == 0, early, late)
    first = jnp.zeros((N_FSDP,), jnp.int32)
    last = jnp.full((N_FSDP,), GROUP_TOK - TOK_DEV // 2, jnp.int32)
    return jnp.stack([first, middle.astype(jnp.int32), last], 1).astype(jnp.int32)


def shard_levels(rng, dims, cuts, low, largest):
    level, own = 1.0, jax.random.fold_in(rng, 6)
    for position, blocks in cuts:
        heights = jnp.exp(jax.random.uniform(jax.random.fold_in(own, position), (blocks,), jnp.float32, low / len(cuts), largest / len(cuts)))
        level = level * jnp.repeat(heights, dims[position] // blocks).reshape([-1 if axis == position else 1 for axis in range(len(dims))])
    return level


def bell_draw(rng, shape, deviation, most, cuts=(), kind=jnp.bfloat16):
    factor_of = shard_levels(rng, shape, cuts, -0.22, 0.18) if cuts else 1.0
    values = jax.random.normal(rng, shape, jnp.float32) * deviation * factor_of
    return jnp.minimum(jnp.maximum(values, -most), most).astype(kind)


def setup_inputs(seed: int = 0) -> dict:
    key_of = jax.random.split(jax.random.key(seed), 10)
    return {
        "tokens": bell_draw(key_of[0], (N_FSDP, GROUP_TOK, D), 1.0, 6.0, ((0, 4), (1, 8))),
        "cotangent": bell_draw(key_of[1], (N_FSDP, GROUP_TOK, D), 1.0, 6.0, ((0, 4), (1, 8))),
        "starts": draw_starts(jax.random.fold_in(key_of[9], 71), 0),
        "w_qkv": bell_draw(key_of[3], (D, 3 * D), D ** -0.5, 0.21875, ((0, 4),)),
        "w_attn": bell_draw(key_of[4], (D, D), (D // 8) ** -0.5, 0.625, ((0, 4),)),
        "w_in": bell_draw(key_of[5], (D, 2 * FF), D ** -0.5, 0.21875, ((0, 4),)),
        "w_out": bell_draw(key_of[6], (FF, D), FF ** -0.5, 0.1875, ((0, 4),)),
        "gain_one": jnp.clip(1.0 + 0.15 * jax.random.normal(key_of[7], (D,), jnp.float32), 0.25, 1.75).astype(jnp.bfloat16),
        "gain_two": jnp.clip(1.0 + 0.15 * jax.random.normal(key_of[8], (D,), jnp.float32), 0.25, 1.75).astype(jnp.bfloat16),
    }


@jax.custom_vjp
def low(v):
    return lax.optimization_barrier(v.astype(jnp.bfloat16)).astype(jnp.float32)

@jax.custom_vjp
def low_back(v):
    return v

def low_keep(v):
    return (low(v), None)

def low_pass(kept, grad):
    return (grad,)

def back_keep(v):
    return (v, None)

def back_low(kept, grad):
    return (low(grad),)
low.defvjp(low_keep, low_pass)
low_back.defvjp(back_keep, back_low)
EPSILON = 1e-05
THETA = 10000.0
HIGHEST = lax.Precision.HIGHEST

def layer_norm(values, gain):
    average = lax.optimization_barrier(jnp.mean(values, -1, keepdims=True))
    centred = values - average
    spread = lax.rsqrt(lax.optimization_barrier(jnp.mean(centred * centred, -1, keepdims=True)) + EPSILON)
    return centred * spread * gain

def rotate(values, cosine, sine):
    middle = values.shape[-1] // 2
    turned = jnp.concatenate([-values[..., middle:], values[..., :middle]], -1)
    return values * cosine + turned * sine

def sequence_tables(starts, length):
    places = jnp.arange(length, dtype=jnp.int32)
    before = starts[:, None, :] <= places[None, :, None]
    idents = (lax.optimization_barrier(jnp.sum(before.astype(jnp.int32), -1)) - 1).astype(jnp.int32)
    first = lax.optimization_barrier(jnp.max(jnp.where(before, starts[:, None, :], 0), -1)).astype(jnp.int32)
    return (idents, places[None, :] - first)

def attend(query, key, value, idents):
    groups, length = (query.shape[0], query.shape[1])
    block = math.gcd(length, 1024)
    span = block + 2 * HALF
    factor = 1.0 / math.sqrt(HD)
    key_pad = jnp.pad(key, ((0, 0), (HALF, HALF), (0, 0), (0, 0)))
    value_pad = jnp.pad(value, ((0, 0), (HALF, HALF), (0, 0), (0, 0)))
    ident_pad = jnp.pad(idents, ((0, 0), (HALF, HALF)), constant_values=-1)
    offsets = jnp.arange(span, dtype=jnp.int32)[None, :] - HALF - jnp.arange(block, dtype=jnp.int32)[:, None]
    nearby = jnp.abs(offsets) <= HALF

    @jax.checkpoint
    def one_block(begin):
        query_block = lax.dynamic_slice_in_dim(query, begin, block, 1)
        key_block = lax.dynamic_slice_in_dim(key_pad, begin, span, 1)
        value_block = lax.dynamic_slice_in_dim(value_pad, begin, span, 1)
        query_ident = lax.dynamic_slice_in_dim(idents, begin, block, 1)
        key_ident = lax.dynamic_slice_in_dim(ident_pad, begin, span, 1)
        allowed = nearby[None, None] & (query_ident[:, None, :, None] == key_ident[:, None, None, :])
        scores = low_back(factor * jnp.einsum('gqhd,gkhd->ghqk', query_block, key_block, precision=HIGHEST))
        masked = jnp.where(allowed, scores, -1e+30)
        highest = lax.optimization_barrier(jnp.max(masked, -1, keepdims=True))
        weights = jnp.where(allowed, jnp.exp(masked - highest), 0.0)
        probs = low(weights / lax.optimization_barrier(jnp.sum(weights, -1, keepdims=True)))
        return jnp.einsum('ghqk,gkhd->gqhd', probs, value_block, precision=HIGHEST)
    beginnings = jnp.arange(length // block, dtype=jnp.int32) * block
    pieces = lax.map(one_block, beginnings)
    return jnp.moveaxis(pieces, 0, 1).reshape(groups, length, HEADS * HD)

def reference(tokens, cotangent, starts, w_qkv, w_attn, w_in, w_out, gain_one, gain_two):
    groups, length, width = tokens.shape
    idents, places = sequence_tables(starts, length)
    freqs = THETA ** (-jnp.arange(HD // 2, dtype=jnp.float32) * 2.0 / HD)
    angles = places.astype(jnp.float32)[..., None] * freqs
    cosine = jnp.concatenate([jnp.cos(angles), jnp.cos(angles)], -1)[:, :, None, :]
    sine = jnp.concatenate([jnp.sin(angles), jnp.sin(angles)], -1)[:, :, None, :]

    def forward(inputs, weight_qkv, weight_attn, weight_in, weight_out, first_gain, second_gain):
        shape_four = (groups, length, HEADS, HD)
        normed = low(layer_norm(inputs, first_gain))
        mixed = low_back(jnp.einsum('gtd,de->gte', normed, weight_qkv, precision=HIGHEST))
        query = low(rotate(mixed[..., :width].reshape(shape_four), cosine, sine))
        key = low(rotate(mixed[..., width:2 * width].reshape(shape_four), cosine, sine))
        value = low(mixed[..., 2 * width:].reshape(shape_four))
        context = low_back(low(attend(query, key, value, idents)))
        attended = low_back(jnp.einsum('gtd,de->gte', context, weight_attn, precision=HIGHEST))
        hidden = inputs + attended
        normed_two = low(layer_norm(hidden, second_gain))
        both = low_back(jnp.einsum('gtd,de->gte', normed_two, weight_in, precision=HIGHEST))
        active = low(jax.nn.gelu(both[..., :FF], approximate=False) * both[..., FF:])
        branch = low_back(jnp.einsum('gtf,fd->gtd', active, weight_out, precision=HIGHEST))
        return hidden + branch
    primals = (tokens.astype(jnp.float32), w_qkv.astype(jnp.float32), w_attn.astype(jnp.float32), w_in.astype(jnp.float32), w_out.astype(jnp.float32), gain_one.astype(jnp.float32), gain_two.astype(jnp.float32))
    output, backward = jax.vjp(forward, *primals)
    grads = backward(cotangent.astype(jnp.float32))
    return (output.astype(jnp.bfloat16), grads[0].astype(jnp.bfloat16), grads[1], grads[2], grads[3], grads[4], grads[5], grads[6])
```

```python
import math

import jax
import jax.numpy as jnp
from jax import lax
from jax.experimental import pallas as pl
from jax.experimental.pallas import tpu as pltpu
from jax.sharding import PartitionSpec as P

HEADS = 12
HALF = 64
BLOCK = 128
SPAN = BLOCK + 2 * HALF
LANES = 128
VMEM_LIMIT = 48 * 1024 * 1024


EPSILON = 1e-05
THETA = 10000.0


def inner_product(left, right):
    return lax.dot_general(
        left, right, (((0,), (0,)), ((), ())), preferred_element_type=jnp.float32
    )


def outer_product(left, right):
    return lax.dot_general(
        left, right, (((1,), (1,)), ((), ())), preferred_element_type=jnp.float32
    )


def norm_parts(values, gain):
    average = jnp.mean(values, -1, keepdims=True)
    centred = values - average
    spread = lax.rsqrt(jnp.mean(centred * centred, -1, keepdims=True) + EPSILON)
    plain = centred * spread
    return (plain, spread, plain * gain)


def norm_back(grad_normed, plain, spread, gain):
    grad_plain = grad_normed * gain
    grad_values = spread * (
        grad_plain
        - jnp.mean(grad_plain, -1, keepdims=True)
        - plain * jnp.mean(grad_plain * plain, -1, keepdims=True)
    )
    return (grad_values, jnp.sum(grad_normed * plain, 0))


def lane_index(rows):
    return lax.broadcasted_iota(jnp.int32, (rows, LANES), 1)


def turned(values, direction):
    first_half = lax.rem(lane_index(values.shape[0]), 64) < 32
    ahead = pltpu.roll(values, LANES - 32, 1)
    behind = pltpu.roll(values, 32, 1)
    return jnp.where(first_half, -direction * ahead, direction * behind)


def pair_rows(values):
    low = lane_index(values.shape[0]) < 64
    zero = jnp.zeros_like(values)
    return jnp.concatenate([jnp.where(low, values, zero), jnp.where(low, zero, values)], 0)


def pair_lanes(stacked):
    rows = stacked.shape[0] // 2
    return jnp.where(lane_index(rows) < 64, stacked[:rows], stacked[rows:])


def attend_kernel(
    bounds, mq, mk, mv, cosine, sine, query, key, value, context, probs, bias_ref
):
    tokens = context.shape[0]
    blocks = tokens // BLOCK
    base = bounds[3]
    group_length = bounds[4]

    @pl.when(pl.program_id(0) == 0)
    def _():
        def ident(place):
            found = jnp.zeros_like(place)
            for index in range(3):
                found = found + (place >= bounds[index]).astype(jnp.int32)
            return jnp.where(place >= group_length, -2, found)

        rows = lax.broadcasted_iota(jnp.int32, (BLOCK, SPAN), 0)
        columns = lax.broadcasted_iota(jnp.int32, (BLOCK, SPAN), 1)
        near = jnp.abs(columns - HALF - rows) <= HALF
        for block in range(blocks):
            begin = base + block * BLOCK
            same = ident(begin + rows) == ident(begin - HALF + columns)
            bias_ref[block] = jnp.where(near & same, 0.0, -1e30)

    table_cos = cosine[...]
    table_sin = sine[...]

    def rope(values):
        return values * table_cos + turned(values, 1.0) * table_sin

    query[...] = rope(mq[...]).astype(jnp.bfloat16)
    key[...] = rope(mk[...]).astype(jnp.bfloat16)
    value[...] = mv[...].astype(jnp.bfloat16)
    for block in range(blocks):
        begin = block * BLOCK
        stacked = pair_rows(query[begin + HALF : begin + HALF + BLOCK] * jnp.bfloat16(0.125))
        keys = key[begin : begin + SPAN]
        scores = lax.dot_general(
            stacked, keys, (((1,), (1,)), ((), ())), preferred_element_type=jnp.float32
        )
        bias = bias_ref[block]
        scores = scores + jnp.concatenate([bias, bias], 0)
        highest = jnp.max(scores, 1, keepdims=True)
        weights = jnp.exp(scores - highest)
        totals = jnp.sum(weights, 1, keepdims=True)
        shares = (weights * (1.0 / totals)).astype(jnp.bfloat16)
        probs[0, block] = shares
        mixed = jnp.dot(shares, value[begin : begin + SPAN], preferred_element_type=jnp.float32)
        context[begin : begin + BLOCK] = pair_lanes(mixed).astype(jnp.bfloat16)


def attend_back_kernel(
    query, key, value, probs, grad_context, cosine, sine, grad_mixed, grad_edges, key_sum, value_sum
):
    tokens = grad_context.shape[0]
    width = grad_mixed.shape[1] // 3
    pair = pl.program_id(0)
    key_sum[...] = jnp.zeros_like(key_sum)
    value_sum[...] = jnp.zeros_like(value_sum)

    def columns(part):
        return pl.ds(pl.multiple_of(part * width + pair * LANES, LANES), LANES)

    def unrope(grads, rows):
        return grads * cosine[rows] - turned(grads, 1.0) * sine[rows]

    for block in range(tokens // BLOCK):
        begin = block * BLOCK
        own = slice(begin + HALF, begin + HALF + BLOCK)
        window = slice(begin, begin + SPAN)
        stacked = pair_rows(query[own] * jnp.bfloat16(0.125))
        grads = pair_rows(grad_context[begin : begin + BLOCK])
        low_probs = probs[0, block]
        shares = low_probs.astype(jnp.float32)
        grad_probs = lax.dot_general(
            grads, value[window], (((1,), (1,)), ((), ())), preferred_element_type=jnp.float32
        )
        delta = jnp.sum(shares * grad_probs, 1, keepdims=True)
        grad_scores = (shares * (grad_probs - delta)).astype(jnp.bfloat16)
        grad_query = pair_lanes(
            jnp.dot(grad_scores, key[window], preferred_element_type=jnp.float32)
        )
        grad_mixed[begin : begin + BLOCK, columns(0)] = unrope(grad_query * 0.125, own).astype(
            jnp.bfloat16
        )
        key_sum[window] += lax.dot_general(
            grad_scores, stacked, (((0,), (0,)), ((), ())), preferred_element_type=jnp.float32
        )
        value_sum[window] += lax.dot_general(
            low_probs, grads, (((0,), (0,)), ((), ())), preferred_element_type=jnp.float32
        )
    everything = slice(0, tokens + 2 * HALF)
    grad_key = unrope(key_sum[...], everything).astype(jnp.bfloat16)
    grad_value = value_sum[...].astype(jnp.bfloat16)
    for part, grads in ((1, grad_key), (2, grad_value)):
        grad_mixed[:, columns(part)] = grads[HALF : HALF + tokens]
        grad_edges[:HALF, columns(part - 1)] = grads[:HALF]
        grad_edges[HALF:, columns(part - 1)] = grads[HALF + tokens :]


def attend(bounds, mixed, cosine, sine, tokens):
    rows, width = mixed.shape[0], mixed.shape[1] // 3
    pairs = width // LANES
    blocks = tokens // BLOCK

    def part(index):
        return pl.BlockSpec((rows, LANES), lambda p, *_: (0, p + index * pairs))

    table = pl.BlockSpec((rows, LANES), lambda p, *_: (0, 0))
    low = lambda count: jax.ShapeDtypeStruct((count, width), jnp.bfloat16)
    return pl.pallas_call(
        attend_kernel,
        grid_spec=pltpu.PrefetchScalarGridSpec(
            num_scalar_prefetch=1,
            grid=(pairs,),
            in_specs=[part(0), part(1), part(2), table, table],
            out_specs=[
                part(0),
                part(0),
                part(0),
                pl.BlockSpec((tokens, LANES), lambda p, *_: (0, p)),
                pl.BlockSpec((1, blocks, 2 * BLOCK, SPAN), lambda p, *_: (p, 0, 0, 0)),
            ],
            scratch_shapes=[pltpu.VMEM((blocks, BLOCK, SPAN), jnp.float32)],
        ),
        out_shape=[
            low(rows),
            low(rows),
            low(rows),
            low(tokens),
            jax.ShapeDtypeStruct((pairs, blocks, 2 * BLOCK, SPAN), jnp.bfloat16),
        ],
        compiler_params=pltpu.CompilerParams(vmem_limit_bytes=VMEM_LIMIT),
        name="attend",
    )(bounds, mixed, mixed, mixed, cosine, sine)


def attend_back(query, key, value, probs, grad_context, cosine, sine):
    tokens, width = grad_context.shape
    rows = query.shape[0]
    pairs = width // LANES
    blocks = tokens // BLOCK
    lanes = pl.BlockSpec((rows, LANES), lambda p: (0, p))
    table = pl.BlockSpec((rows, LANES), lambda p: (0, 0))
    return pl.pallas_call(
        attend_back_kernel,
        grid=(pairs,),
        in_specs=[
            lanes,
            lanes,
            lanes,
            pl.BlockSpec((1, blocks, 2 * BLOCK, SPAN), lambda p: (p, 0, 0, 0)),
            pl.BlockSpec((tokens, LANES), lambda p: (0, p)),
            table,
            table,
        ],
        out_specs=[
            pl.BlockSpec((tokens, 3 * width), lambda p: (0, 0)),
            pl.BlockSpec((2 * HALF, 2 * width), lambda p: (0, 0)),
        ],
        out_shape=[
            jax.ShapeDtypeStruct((tokens, 3 * width), jnp.bfloat16),
            jax.ShapeDtypeStruct((2 * HALF, 2 * width), jnp.bfloat16),
        ],
        scratch_shapes=[
            pltpu.VMEM((rows, LANES), jnp.float32),
            pltpu.VMEM((rows, LANES), jnp.float32),
        ],
        compiler_params=pltpu.CompilerParams(vmem_limit_bytes=VMEM_LIMIT),
        name="attend_back",
    )(query, key, value, probs, grad_context, cosine, sine)


def passed_along(value, axis, steps):
    count = lax.axis_size(axis)
    first, last = (max(0, -steps), min(count, count - steps))
    return lax.ppermute(value, axis, [(source, source + steps) for source in range(first, last)])


def summed_rows(partial):
    rows = lax.psum_scatter(
        partial.astype(jnp.bfloat16), "fsdp", scatter_dimension=0, tiled=True
    )
    count = rows.shape[0]
    padding = -count % (8 * lax.axis_size("seq"))
    if padding:
        rows = jnp.pad(rows, ((0, padding), (0, 0)))
    share = lax.psum_scatter(rows, "seq", scatter_dimension=0, tiled=True)
    return lax.all_gather(share, "seq", axis=0, tiled=True)[:count].astype(jnp.float32)


def body(tokens, cotangent, starts, w_qkv, w_attn, w_in, w_out, gain_one, gain_two):
    tok_count, model_width = tokens.shape[1:]
    head_size = model_width // HEADS
    before = passed_along(tokens[0, tok_count - HALF :], "seq", 1)
    after = passed_along(tokens[0, :HALF], "seq", -1)
    gains = lax.all_gather(jnp.stack([gain_one, gain_two]), "fsdp", axis=1, tiled=True)
    full_qkv, full_attn, full_in, full_out = (
        lax.all_gather(w_qkv, "fsdp", axis=0, tiled=True),
        lax.all_gather(w_attn, "fsdp", axis=0, tiled=True),
        lax.all_gather(w_in, "fsdp", axis=0, tiled=True),
        lax.all_gather(w_out, "fsdp", axis=0, tiled=True),
    )
    first_gain = gains[0].astype(jnp.float32)
    second_gain = gains[1].astype(jnp.float32)
    extended = jnp.concatenate([before, tokens[0], after], 0).astype(jnp.float32)
    inputs = tokens[0].astype(jnp.float32)
    ff_width = full_out.shape[0]
    seq_index = lax.axis_index("seq")
    group_length = tok_count * lax.axis_size("seq")
    seq_starts = starts[0]
    places = seq_index * tok_count - HALF + jnp.arange(tok_count + 2 * HALF, dtype=jnp.int32)
    earlier = seq_starts[None, :] <= places[:, None]
    first_token = jnp.max(jnp.where(earlier, seq_starts[None, :], 0), 1)
    position = (places - first_token).astype(jnp.float32)
    freqs = THETA ** (-jnp.arange(head_size // 2, dtype=jnp.float32) * 2.0 / head_size)
    angles = position[:, None] * freqs[None, :]
    cosine = jnp.tile(jnp.cos(angles), (1, LANES // (head_size // 2)))
    sine = jnp.tile(jnp.sin(angles), (1, LANES // (head_size // 2)))
    bounds = jnp.concatenate(
        [
            seq_starts,
            jnp.stack([seq_index * tok_count, jnp.int32(group_length)]).astype(jnp.int32),
        ]
    )
    normed_ext = norm_parts(extended, first_gain)[2].astype(jnp.bfloat16)
    mixed = jnp.dot(normed_ext, full_qkv, preferred_element_type=jnp.float32)
    query, key, value, context, probs = attend(bounds, mixed, cosine, sine, tok_count)
    hidden = inputs + jnp.dot(context, full_attn, preferred_element_type=jnp.float32)
    plain_two, spread_two, normed_two = norm_parts(hidden, second_gain)
    normed_two_low = normed_two.astype(jnp.bfloat16)
    both = jnp.dot(normed_two_low, full_in, preferred_element_type=jnp.float32)
    gate = both[:, :ff_width]
    upper = both[:, ff_width:]
    active, gelu_back = jax.vjp(lambda entry: jax.nn.gelu(entry, approximate=False), gate)
    act_low = (active * upper).astype(jnp.bfloat16)
    output = hidden + jnp.dot(act_low, full_out, preferred_element_type=jnp.float32)
    grad_result = cotangent[0]
    grad_wout = inner_product(act_low, grad_result)
    grad_act = outer_product(grad_result, full_out)
    grad_gate = gelu_back(grad_act * upper)[0]
    grad_both = jnp.concatenate([grad_gate, grad_act * active], 1).astype(jnp.bfloat16)
    grad_win = inner_product(normed_two_low, grad_both)
    grad_normed_two = outer_product(grad_both, full_in)
    grad_hidden_norm, grad_second = norm_back(grad_normed_two, plain_two, spread_two, second_gain)
    grad_hidden = grad_result.astype(jnp.float32) + grad_hidden_norm
    grad_hidden_low = grad_hidden.astype(jnp.bfloat16)
    grad_wattn = inner_product(context, grad_hidden_low)
    grad_context = outer_product(grad_hidden_low, full_attn).astype(jnp.bfloat16)

    grad_mixed, grad_edges = attend_back(query, key, value, probs, grad_context, cosine, sine)
    from_lower = passed_along(grad_edges[HALF:], "seq", 1)
    from_upper = passed_along(grad_edges[:HALF], "seq", -1)
    grad_mixed = grad_mixed.at[:HALF, model_width:].add(from_lower)
    grad_mixed = grad_mixed.at[tok_count - HALF :, model_width:].add(from_upper)
    normed_low = normed_ext[HALF : HALF + tok_count]
    plain_one, spread_one, _ = norm_parts(inputs, first_gain)
    grad_wqkv = inner_product(normed_low, grad_mixed)
    grad_normed_one = outer_product(grad_mixed, full_qkv)
    grad_input_norm, grad_first = norm_back(grad_normed_one, plain_one, spread_one, first_gain)
    grad_inputs = (grad_hidden + grad_input_norm).astype(jnp.bfloat16)
    sums = lax.psum(jnp.stack([grad_first, grad_second]), ("seq", "fsdp"))
    rows = gain_one.shape[0]
    own_gains = lax.dynamic_slice_in_dim(sums, lax.axis_index("fsdp") * rows, rows, 1)
    return (
        output.astype(jnp.bfloat16)[None],
        grad_inputs[None],
        summed_rows(grad_wqkv),
        summed_rows(grad_wattn),
        summed_rows(grad_win),
        summed_rows(grad_wout),
        own_gains[0],
        own_gains[1],
    )


def solution(mesh):
    in_specs = (
        P("fsdp", "seq", None),
        P("fsdp", "seq", None),
        P("fsdp", None),
        P("fsdp", None),
        P("fsdp", None),
        P("fsdp", None),
        P("fsdp", None),
        P("fsdp"),
        P("fsdp"),
    )
    out_specs = (
        P("fsdp", "seq", None),
        P("fsdp", "seq", None),
        P("fsdp", None),
        P("fsdp", None),
        P("fsdp", None),
        P("fsdp", None),
        P("fsdp"),
        P("fsdp"),
    )
    return jax.shard_map(body, mesh=mesh, in_specs=in_specs, out_specs=out_specs, check_vma=False)
```

```python
import math

import jax
import jax.numpy as jnp
from jax import lax
from jax.experimental import pallas as pl
from jax.experimental.pallas import tpu as pltpu
from jax.sharding import PartitionSpec as P

HEADS = 12
HALF = 64
BLOCK = 128
SPAN = BLOCK + 2 * HALF
LANES = 128
VMEM_LIMIT = 48 * 1024 * 1024


EPSILON = 1e-05
THETA = 10000.0


def inner_product(left, right):
    return lax.dot_general(
        left, right, (((0,), (0,)), ((), ())), preferred_element_type=jnp.float32
    )


def outer_product(left, right):
    return lax.dot_general(
        left, right, (((1,), (1,)), ((), ())), preferred_element_type=jnp.float32
    )


def norm_parts(values, gain):
    average = jnp.mean(values, -1, keepdims=True)
    centred = values - average
    spread = lax.rsqrt(jnp.mean(centred * centred, -1, keepdims=True) + EPSILON)
    plain = centred * spread
    return (plain, spread, plain * gain)


def norm_back(grad_normed, plain, spread, gain):
    grad_plain = grad_normed * gain
    grad_values = spread * (
        grad_plain
        - jnp.mean(grad_plain, -1, keepdims=True)
        - plain * jnp.mean(grad_plain * plain, -1, keepdims=True)
    )
    return (grad_values, jnp.sum(grad_normed * plain, 0))


def lane_index(rows):
    return lax.broadcasted_iota(jnp.int32, (rows, LANES), 1)


def turned(values, direction):
    first_half = lax.rem(lane_index(values.shape[0]), 64) < 32
    ahead = pltpu.roll(values, LANES - 32, 1)
    behind = pltpu.roll(values, 32, 1)
    return jnp.where(first_half, -direction * ahead, direction * behind)


def pair_rows(values):
    low = lane_index(values.shape[0]) < 64
    zero = jnp.zeros_like(values)
    return jnp.concatenate([jnp.where(low, values, zero), jnp.where(low, zero, values)], 0)


def pair_lanes(stacked):
    rows = stacked.shape[0] // 2
    return jnp.where(lane_index(rows) < 64, stacked[:rows], stacked[rows:])


def attend_kernel(
    bounds, mq, mk, mv, cosine, sine, query, key, value, context, probs, bias_ref
):
    tokens = context.shape[0]
    blocks = tokens // BLOCK
    base = bounds[3]
    group_length = bounds[4]

    @pl.when(pl.program_id(0) == 0)
    def _():
        def ident(place):
            found = jnp.zeros_like(place)
            for index in range(3):
                found = found + (place >= bounds[index]).astype(jnp.int32)
            return jnp.where(place >= group_length, -2, found)

        rows = lax.broadcasted_iota(jnp.int32, (BLOCK, SPAN), 0)
        columns = lax.broadcasted_iota(jnp.int32, (BLOCK, SPAN), 1)
        near = jnp.abs(columns - HALF - rows) <= HALF
        for block in range(blocks):
            begin = base + block * BLOCK
            same = ident(begin + rows) == ident(begin - HALF + columns)
            bias_ref[block] = jnp.where(near & same, 0.0, -1e30)

    table_cos = cosine[...]
    table_sin = sine[...]

    def rope(values):
        return values * table_cos + turned(values, 1.0) * table_sin

    query[...] = rope(mq[...]).astype(jnp.bfloat16)
    key[...] = rope(mk[...]).astype(jnp.bfloat16)
    value[...] = mv[...].astype(jnp.bfloat16)
    for block in range(blocks):
        begin = block * BLOCK
        stacked = pair_rows(query[begin + HALF : begin + HALF + BLOCK] * jnp.bfloat16(0.125))
        keys = key[begin : begin + SPAN]
        scores = lax.dot_general(
            stacked, keys, (((1,), (1,)), ((), ())), preferred_element_type=jnp.float32
        )
        bias = bias_ref[block]
        scores = scores + jnp.concatenate([bias, bias], 0)
        highest = jnp.max(scores, 1, keepdims=True)
        weights = jnp.exp(scores - highest)
        totals = jnp.sum(weights, 1, keepdims=True)
        shares = (weights * (1.0 / totals)).astype(jnp.bfloat16)
        probs[0, block] = shares
        mixed = jnp.dot(shares, value[begin : begin + SPAN], preferred_element_type=jnp.float32)
        context[begin : begin + BLOCK] = pair_lanes(mixed).astype(jnp.bfloat16)


def attend_back_kernel(
    query, key, value, probs, grad_context, cosine, sine, grad_mixed, grad_edges, key_sum, value_sum
):
    tokens = grad_context.shape[0]
    width = grad_mixed.shape[1] // 3
    pair = pl.program_id(0)
    key_sum[...] = jnp.zeros_like(key_sum)
    value_sum[...] = jnp.zeros_like(value_sum)

    def columns(part):
        return pl.ds(pl.multiple_of(part * width + pair * LANES, LANES), LANES)

    def unrope(grads, rows):
        return grads * cosine[rows] - turned(grads, 1.0) * sine[rows]

    for block in range(tokens // BLOCK):
        begin = block * BLOCK
        own = slice(begin + HALF, begin + HALF + BLOCK)
        window = slice(begin, begin + SPAN)
        stacked = pair_rows(query[own] * jnp.bfloat16(0.125))
        grads = pair_rows(grad_context[begin : begin + BLOCK])
        low_probs = probs[0, block]
        shares = low_probs.astype(jnp.float32)
        grad_probs = lax.dot_general(
            grads, value[window], (((1,), (1,)), ((), ())), preferred_element_type=jnp.float32
        )
        delta = jnp.sum(shares * grad_probs, 1, keepdims=True)
        grad_scores = (shares * (grad_probs - delta)).astype(jnp.bfloat16)
        grad_query = pair_lanes(
            jnp.dot(grad_scores, key[window], preferred_element_type=jnp.float32)
        )
        grad_mixed[begin : begin + BLOCK, columns(0)] = unrope(grad_query * 0.125, own).astype(
            jnp.bfloat16
        )
        key_sum[window] += lax.dot_general(
            grad_scores, stacked, (((0,), (0,)), ((), ())), preferred_element_type=jnp.float32
        )
        value_sum[window] += lax.dot_general(
            low_probs, grads, (((0,), (0,)), ((), ())), preferred_element_type=jnp.float32
        )
    everything = slice(0, tokens + 2 * HALF)
    grad_key = unrope(key_sum[...], everything).astype(jnp.bfloat16)
    grad_value = value_sum[...].astype(jnp.bfloat16)
    for part, grads in ((1, grad_key), (2, grad_value)):
        grad_mixed[:, columns(part)] = grads[HALF : HALF + tokens]
        grad_edges[:HALF, columns(part - 1)] = grads[:HALF]
        grad_edges[HALF:, columns(part - 1)] = grads[HALF + tokens :]


def attend(bounds, mixed, cosine, sine, tokens):
    rows, width = mixed.shape[0], mixed.shape[1] // 3
    pairs = width // LANES
    blocks = tokens // BLOCK

    def part(index):
        return pl.BlockSpec((rows, LANES), lambda p, *_: (0, p + index * pairs))

    table = pl.BlockSpec((rows, LANES), lambda p, *_: (0, 0))
    low = lambda count: jax.ShapeDtypeStruct((count, width), jnp.bfloat16)
    return pl.pallas_call(
        attend_kernel,
        grid_spec=pltpu.PrefetchScalarGridSpec(
            num_scalar_prefetch=1,
            grid=(pairs,),
            in_specs=[part(0), part(1), part(2), table, table],
            out_specs=[
                part(0),
                part(0),
                part(0),
                pl.BlockSpec((tokens, LANES), lambda p, *_: (0, p)),
                pl.BlockSpec((1, blocks, 2 * BLOCK, SPAN), lambda p, *_: (p, 0, 0, 0)),
            ],
            scratch_shapes=[pltpu.VMEM((blocks, BLOCK, SPAN), jnp.float32)],
        ),
        out_shape=[
            low(rows),
            low(rows),
            low(rows),
            low(tokens),
            jax.ShapeDtypeStruct((pairs, blocks, 2 * BLOCK, SPAN), jnp.bfloat16),
        ],
        compiler_params=pltpu.CompilerParams(vmem_limit_bytes=VMEM_LIMIT),
        cost_estimate=pl.CostEstimate(
            flops=20000 * tokens * width, bytes_accessed=50 * tokens * width, transcendentals=0
        ),
        name="attend",
    )(bounds, mixed, mixed, mixed, cosine, sine)


def attend_back(query, key, value, probs, grad_context, cosine, sine):
    tokens, width = grad_context.shape
    rows = query.shape[0]
    pairs = width // LANES
    blocks = tokens // BLOCK
    lanes = pl.BlockSpec((rows, LANES), lambda p: (0, p))
    table = pl.BlockSpec((rows, LANES), lambda p: (0, 0))
    return pl.pallas_call(
        attend_back_kernel,
        grid=(pairs,),
        in_specs=[
            lanes,
            lanes,
            lanes,
            pl.BlockSpec((1, blocks, 2 * BLOCK, SPAN), lambda p: (p, 0, 0, 0)),
            pl.BlockSpec((tokens, LANES), lambda p: (0, p)),
            table,
            table,
        ],
        out_specs=[
            pl.BlockSpec((tokens, 3 * width), lambda p: (0, 0)),
            pl.BlockSpec((2 * HALF, 2 * width), lambda p: (0, 0)),
        ],
        out_shape=[
            jax.ShapeDtypeStruct((tokens, 3 * width), jnp.bfloat16),
            jax.ShapeDtypeStruct((2 * HALF, 2 * width), jnp.bfloat16),
        ],
        scratch_shapes=[
            pltpu.VMEM((rows, LANES), jnp.float32),
            pltpu.VMEM((rows, LANES), jnp.float32),
        ],
        compiler_params=pltpu.CompilerParams(vmem_limit_bytes=VMEM_LIMIT),
        cost_estimate=pl.CostEstimate(
            flops=30000 * tokens * width, bytes_accessed=50 * tokens * width, transcendentals=0
        ),
        name="attend_back",
    )(query, key, value, probs, grad_context, cosine, sine)


def passed_along(value, axis, steps):
    count = lax.axis_size(axis)
    first, last = (max(0, -steps), min(count, count - steps))
    return lax.ppermute(value, axis, [(source, source + steps) for source in range(first, last)])


def swapped(value, axis, mask):
    return lax.ppermute(value, axis, [(i, i ^ mask) for i in range(lax.axis_size(axis))])


def place_bits(axis):
    index, bits, mask = lax.axis_index(axis), [], 1
    while mask < lax.axis_size(axis):
        bits.append((mask, lax.rem(index // mask, 2)))
        mask *= 2
    return bits


def halved(parts, dim, axis, mask, bit):
    kept = lax.dynamic_index_in_dim(parts, bit, dim, keepdims=False)
    sent = lax.dynamic_index_in_dim(parts, 1 - bit, dim, keepdims=False)
    got = swapped(sent, axis, mask)
    return (kept.astype(jnp.float32) + got.astype(jnp.float32)).astype(jnp.bfloat16)


def padded_rows(parts):
    padding = -parts.shape[1] % (8 * lax.axis_size("seq"))
    return jnp.pad(parts, ((0, 0), (0, padding), (0, 0))) if padding else parts


def summed_shards(parts, bits):
    for mask, bit in bits:
        shards, rows, columns = parts.shape
        parts = halved(parts.reshape(shards // 2, 2, rows, columns), 1, "fsdp", mask, bit)
    return parts


def summed_rows(share):
    bits = place_bits("seq")
    for mask, bit in bits:
        rows, columns = share.shape
        share = halved(share.reshape(2, rows // 2, columns), 0, "seq", mask, bit)
    for mask, bit in reversed(bits):
        other = swapped(share, "seq", mask)
        share = jnp.where(
            bit == 0, jnp.concatenate([share, other], 0), jnp.concatenate([other, share], 0)
        )
    return share


def body(tokens, cotangent, starts, w_qkv, w_attn, w_in, w_out, gain_one, gain_two):
    tok_count, model_width = tokens.shape[1:]
    head_size = model_width // HEADS
    before = passed_along(tokens[0, tok_count - HALF :], "seq", 1)
    after = passed_along(tokens[0, :HALF], "seq", -1)
    gains = lax.all_gather(jnp.stack([gain_one, gain_two]), "fsdp", axis=1, tiled=True)
    full_qkv, full_attn, full_in, full_out = (
        lax.all_gather(w_qkv, "fsdp", axis=0, tiled=True),
        lax.all_gather(w_attn, "fsdp", axis=0, tiled=True),
        lax.all_gather(w_in, "fsdp", axis=0, tiled=True),
        lax.all_gather(w_out, "fsdp", axis=0, tiled=True),
    )
    first_gain = gains[0].astype(jnp.float32)
    second_gain = gains[1].astype(jnp.float32)
    extended = jnp.concatenate([before, tokens[0], after], 0).astype(jnp.float32)
    inputs = tokens[0].astype(jnp.float32)
    ff_width = full_out.shape[0]
    seq_index = lax.axis_index("seq")
    group_length = tok_count * lax.axis_size("seq")
    seq_starts = starts[0]
    places = seq_index * tok_count - HALF + jnp.arange(tok_count + 2 * HALF, dtype=jnp.int32)
    earlier = seq_starts[None, :] <= places[:, None]
    first_token = jnp.max(jnp.where(earlier, seq_starts[None, :], 0), 1)
    position = (places - first_token).astype(jnp.float32)
    freqs = THETA ** (-jnp.arange(head_size // 2, dtype=jnp.float32) * 2.0 / head_size)
    angles = position[:, None] * freqs[None, :]
    cosine = jnp.tile(jnp.cos(angles), (1, LANES // (head_size // 2)))
    sine = jnp.tile(jnp.sin(angles), (1, LANES // (head_size // 2)))
    bounds = jnp.concatenate(
        [
            seq_starts,
            jnp.stack([seq_index * tok_count, jnp.int32(group_length)]).astype(jnp.int32),
        ]
    )
    normed_ext = norm_parts(extended, first_gain)[2].astype(jnp.bfloat16)
    mixed = jnp.dot(normed_ext, full_qkv, preferred_element_type=jnp.float32)
    query, key, value, context, probs = attend(bounds, mixed, cosine, sine, tok_count)
    hidden = inputs + jnp.dot(context, full_attn, preferred_element_type=jnp.float32)
    plain_two, spread_two, normed_two = norm_parts(hidden, second_gain)
    normed_two_low = normed_two.astype(jnp.bfloat16)
    both = jnp.dot(normed_two_low, full_in, preferred_element_type=jnp.float32)
    gate = both[:, :ff_width]
    upper = both[:, ff_width:]
    active, gelu_back = jax.vjp(lambda entry: jax.nn.gelu(entry, approximate=False), gate)
    act_low = (active * upper).astype(jnp.bfloat16)
    output = hidden + jnp.dot(act_low, full_out, preferred_element_type=jnp.float32)
    grad_result = cotangent[0]
    grad_wout = inner_product(act_low, grad_result)
    grad_act = outer_product(grad_result, full_out)
    grad_gate = gelu_back(grad_act * upper)[0]
    grad_both = jnp.concatenate([grad_gate, grad_act * active], 1).astype(jnp.bfloat16)
    grad_win = inner_product(normed_two_low, grad_both)
    grad_normed_two = outer_product(grad_both, full_in)
    grad_hidden_norm, grad_second = norm_back(grad_normed_two, plain_two, spread_two, second_gain)
    grad_hidden = grad_result.astype(jnp.float32) + grad_hidden_norm
    grad_hidden_low = grad_hidden.astype(jnp.bfloat16)
    grad_wattn = inner_product(context, grad_hidden_low)
    grad_context = outer_product(grad_hidden_low, full_attn).astype(jnp.bfloat16)

    shards = lax.axis_size("fsdp")

    def by_shard(grads):
        return grads.astype(jnp.bfloat16).reshape(shards, grads.shape[0] // shards, grads.shape[1])

    win_parts = by_shard(grad_win)
    early_parts = [
        win_parts[..., begin : begin + model_width]
        for begin in range(0, win_parts.shape[2], model_width)
    ] + [by_shard(grad_wattn), by_shard(grad_wout)]
    bits = place_bits("fsdp")
    early = summed_shards(padded_rows(jnp.concatenate(early_parts, 1)), bits[:1])
    early, grad_context = lax.optimization_barrier((early, grad_context))
    early = summed_shards(early, bits[1:])
    grad_mixed, grad_edges = attend_back(query, key, value, probs, grad_context, cosine, sine)
    from_lower = passed_along(grad_edges[HALF:], "seq", 1)
    from_upper = passed_along(grad_edges[:HALF], "seq", -1)
    grad_mixed = grad_mixed.at[:HALF, model_width:].add(from_lower)
    grad_mixed = grad_mixed.at[tok_count - HALF :, model_width:].add(from_upper)
    early, grad_mixed = lax.optimization_barrier((early, grad_mixed))
    early = summed_rows(early[0]).astype(jnp.float32)
    early_sums, begin = [], 0
    for piece in early_parts:
        early_sums.append(early[begin : begin + piece.shape[1]])
        begin += piece.shape[1]
    normed_low = normed_ext[HALF : HALF + tok_count]
    plain_one, spread_one, _ = norm_parts(inputs, first_gain)
    grad_wqkv = inner_product(normed_low, grad_mixed)
    late = summed_rows(summed_shards(padded_rows(by_shard(grad_wqkv)), bits)[0])
    grad_normed_one = outer_product(grad_mixed, full_qkv)
    grad_input_norm, grad_first = norm_back(grad_normed_one, plain_one, spread_one, first_gain)
    grad_inputs = (grad_hidden + grad_input_norm).astype(jnp.bfloat16)
    sums = lax.psum(jnp.stack([grad_first, grad_second]), ("seq", "fsdp"))
    rows = gain_one.shape[0]
    own_gains = lax.dynamic_slice_in_dim(sums, lax.axis_index("fsdp") * rows, rows, 1)
    return (
        output.astype(jnp.bfloat16)[None],
        grad_inputs[None],
        late[: w_qkv.shape[0]].astype(jnp.float32),
        early_sums[-2],
        jnp.concatenate(early_sums[:-2], 1),
        early_sums[-1],
        own_gains[0],
        own_gains[1],
    )


def solution(mesh):
    in_specs = (
        P("fsdp", "seq", None),
        P("fsdp", "seq", None),
        P("fsdp", None),
        P("fsdp", None),
        P("fsdp", None),
        P("fsdp", None),
        P("fsdp", None),
        P("fsdp"),
        P("fsdp"),
    )
    out_specs = (
        P("fsdp", "seq", None),
        P("fsdp", "seq", None),
        P("fsdp", None),
        P("fsdp", None),
        P("fsdp", None),
        P("fsdp", None),
        P("fsdp"),
        P("fsdp"),
    )
    return jax.shard_map(body, mesh=mesh, in_specs=in_specs, out_specs=out_specs, check_vma=False)
```

```python
import math

import jax
import jax.numpy as jnp
from jax import lax
from jax.experimental import pallas as pl
from jax.experimental.pallas import tpu as pltpu
from jax.sharding import PartitionSpec as P

HEADS = 12
HALF = 64
BLOCK = 128
SPAN = BLOCK + 2 * HALF
LANES = 128
VMEM_LIMIT = 48 * 1024 * 1024


EPSILON = 1e-05
THETA = 10000.0


def inner_product(left, right):
    return lax.dot_general(
        left, right, (((0,), (0,)), ((), ())), preferred_element_type=jnp.float32
    )


def outer_product(left, right):
    return lax.dot_general(
        left, right, (((1,), (1,)), ((), ())), preferred_element_type=jnp.float32
    )


def norm_parts(values, gain):
    average = jnp.mean(values, -1, keepdims=True)
    centred = values - average
    spread = lax.rsqrt(jnp.mean(centred * centred, -1, keepdims=True) + EPSILON)
    plain = centred * spread
    return (plain, spread, plain * gain)


def norm_back(grad_normed, plain, spread, gain):
    grad_plain = grad_normed * gain
    grad_values = spread * (
        grad_plain
        - jnp.mean(grad_plain, -1, keepdims=True)
        - plain * jnp.mean(grad_plain * plain, -1, keepdims=True)
    )
    return (grad_values, jnp.sum(grad_normed * plain, 0))


def lane_index(rows):
    return lax.broadcasted_iota(jnp.int32, (rows, LANES), 1)


def turned(values, direction):
    first_half = lax.rem(lane_index(values.shape[0]), 64) < 32
    ahead = pltpu.roll(values, LANES - 32, 1)
    behind = pltpu.roll(values, 32, 1)
    return jnp.where(first_half, -direction * ahead, direction * behind)


def pair_rows(values):
    low = lane_index(values.shape[0]) < 64
    zero = jnp.zeros_like(values)
    return jnp.concatenate([jnp.where(low, values, zero), jnp.where(low, zero, values)], 0)


def pair_lanes(stacked):
    rows = stacked.shape[0] // 2
    return jnp.where(lane_index(rows) < 64, stacked[:rows], stacked[rows:])


def attend_kernel(
    bounds, mq, mk, mv, cosine, sine, query, key, value, context, probs, bias_ref
):
    tokens = context.shape[0]
    blocks = tokens // BLOCK
    base = bounds[3]
    group_length = bounds[4]

    @pl.when(pl.program_id(0) == 0)
    def _():
        def ident(place):
            found = jnp.zeros_like(place)
            for index in range(3):
                found = found + (place >= bounds[index]).astype(jnp.int32)
            return jnp.where(place >= group_length, -2, found)

        rows = lax.broadcasted_iota(jnp.int32, (BLOCK, SPAN), 0)
        columns = lax.broadcasted_iota(jnp.int32, (BLOCK, SPAN), 1)
        near = jnp.abs(columns - HALF - rows) <= HALF
        for block in range(blocks):
            begin = base + block * BLOCK
            same = ident(begin + rows) == ident(begin - HALF + columns)
            bias_ref[block] = jnp.where(near & same, 0.0, -1e30)

    table_cos = cosine[...]
    table_sin = sine[...]

    def rope(values):
        return values * table_cos + turned(values, 1.0) * table_sin

    query[...] = rope(mq[...]).astype(jnp.bfloat16)
    key[...] = rope(mk[...]).astype(jnp.bfloat16)
    value[...] = mv[...].astype(jnp.bfloat16)
    for block in range(blocks):
        begin = block * BLOCK
        stacked = pair_rows(query[begin + HALF : begin + HALF + BLOCK] * jnp.bfloat16(0.125))
        keys = key[begin : begin + SPAN]
        scores = lax.dot_general(
            stacked, keys, (((1,), (1,)), ((), ())), preferred_element_type=jnp.float32
        )
        bias = bias_ref[block]
        scores = scores + jnp.concatenate([bias, bias], 0)
        highest = jnp.max(scores, 1, keepdims=True)
        weights = jnp.exp(scores - highest)
        totals = jnp.sum(weights, 1, keepdims=True)
        shares = (weights * (1.0 / totals)).astype(jnp.bfloat16)
        probs[0, block] = shares
        mixed = jnp.dot(shares, value[begin : begin + SPAN], preferred_element_type=jnp.float32)
        context[begin : begin + BLOCK] = pair_lanes(mixed).astype(jnp.bfloat16)


def attend_back_kernel(
    query, key, value, probs, grad_context, cosine, sine, grad_mixed, grad_edges, key_sum, value_sum
):
    tokens = grad_context.shape[0]
    width = grad_mixed.shape[1] // 3
    pair = pl.program_id(0)
    key_sum[...] = jnp.zeros_like(key_sum)
    value_sum[...] = jnp.zeros_like(value_sum)

    def columns(part):
        return pl.ds(pl.multiple_of(part * width + pair * LANES, LANES), LANES)

    def unrope(grads, rows):
        return grads * cosine[rows] - turned(grads, 1.0) * sine[rows]

    for block in range(tokens // BLOCK):
        begin = block * BLOCK
        own = slice(begin + HALF, begin + HALF + BLOCK)
        window = slice(begin, begin + SPAN)
        stacked = pair_rows(query[own] * jnp.bfloat16(0.125))
        grads = pair_rows(grad_context[begin : begin + BLOCK])
        low_probs = probs[0, block]
        shares = low_probs.astype(jnp.float32)
        grad_probs = lax.dot_general(
            grads, value[window], (((1,), (1,)), ((), ())), preferred_element_type=jnp.float32
        )
        delta = jnp.sum(shares * grad_probs, 1, keepdims=True)
        grad_scores = (shares * (grad_probs - delta)).astype(jnp.bfloat16)
        grad_query = pair_lanes(
            jnp.dot(grad_scores, key[window], preferred_element_type=jnp.float32)
        )
        grad_mixed[begin : begin + BLOCK, columns(0)] = unrope(grad_query * 0.125, own).astype(
            jnp.bfloat16
        )
        key_sum[window] += lax.dot_general(
            grad_scores, stacked, (((0,), (0,)), ((), ())), preferred_element_type=jnp.float32
        )
        value_sum[window] += lax.dot_general(
            low_probs, grads, (((0,), (0,)), ((), ())), preferred_element_type=jnp.float32
        )
    everything = slice(0, tokens + 2 * HALF)
    grad_key = unrope(key_sum[...], everything).astype(jnp.bfloat16)
    grad_value = value_sum[...].astype(jnp.bfloat16)
    for part, grads in ((1, grad_key), (2, grad_value)):
        grad_mixed[:, columns(part)] = grads[HALF : HALF + tokens]
        grad_edges[:HALF, columns(part - 1)] = grads[:HALF]
        grad_edges[HALF:, columns(part - 1)] = grads[HALF + tokens :]


def attend(bounds, mixed, cosine, sine, tokens):
    rows, width = mixed.shape[0], mixed.shape[1] // 3
    pairs = width // LANES
    blocks = tokens // BLOCK

    def part(index):
        return pl.BlockSpec((rows, LANES), lambda p, *_: (0, p + index * pairs))

    table = pl.BlockSpec((rows, LANES), lambda p, *_: (0, 0))
    low = lambda count: jax.ShapeDtypeStruct((count, width), jnp.bfloat16)
    return pl.pallas_call(
        attend_kernel,
        grid_spec=pltpu.PrefetchScalarGridSpec(
            num_scalar_prefetch=1,
            grid=(pairs,),
            in_specs=[part(0), part(1), part(2), table, table],
            out_specs=[
                part(0),
                part(0),
                part(0),
                pl.BlockSpec((tokens, LANES), lambda p, *_: (0, p)),
                pl.BlockSpec((1, blocks, 2 * BLOCK, SPAN), lambda p, *_: (p, 0, 0, 0)),
            ],
            scratch_shapes=[pltpu.VMEM((blocks, BLOCK, SPAN), jnp.float32)],
        ),
        out_shape=[
            low(rows),
            low(rows),
            low(rows),
            low(tokens),
            jax.ShapeDtypeStruct((pairs, blocks, 2 * BLOCK, SPAN), jnp.bfloat16),
        ],
        compiler_params=pltpu.CompilerParams(vmem_limit_bytes=VMEM_LIMIT),
        cost_estimate=pl.CostEstimate(
            flops=20000 * tokens * width, bytes_accessed=50 * tokens * width, transcendentals=0
        ),
        name="attend",
    )(bounds, mixed, mixed, mixed, cosine, sine)


def attend_back(query, key, value, probs, grad_context, cosine, sine):
    tokens, width = grad_context.shape
    rows = query.shape[0]
    pairs = width // LANES
    blocks = tokens // BLOCK
    lanes = pl.BlockSpec((rows, LANES), lambda p: (0, p))
    table = pl.BlockSpec((rows, LANES), lambda p: (0, 0))
    return pl.pallas_call(
        attend_back_kernel,
        grid=(pairs,),
        in_specs=[
            lanes,
            lanes,
            lanes,
            pl.BlockSpec((1, blocks, 2 * BLOCK, SPAN), lambda p: (p, 0, 0, 0)),
            pl.BlockSpec((tokens, LANES), lambda p: (0, p)),
            table,
            table,
        ],
        out_specs=[
            pl.BlockSpec((tokens, 3 * width), lambda p: (0, 0)),
            pl.BlockSpec((2 * HALF, 2 * width), lambda p: (0, 0)),
        ],
        out_shape=[
            jax.ShapeDtypeStruct((tokens, 3 * width), jnp.bfloat16),
            jax.ShapeDtypeStruct((2 * HALF, 2 * width), jnp.bfloat16),
        ],
        scratch_shapes=[
            pltpu.VMEM((rows, LANES), jnp.float32),
            pltpu.VMEM((rows, LANES), jnp.float32),
        ],
        compiler_params=pltpu.CompilerParams(vmem_limit_bytes=VMEM_LIMIT),
        cost_estimate=pl.CostEstimate(
            flops=30000 * tokens * width, bytes_accessed=50 * tokens * width, transcendentals=0
        ),
        name="attend_back",
    )(query, key, value, probs, grad_context, cosine, sine)


def passed_along(value, axis, steps):
    count = lax.axis_size(axis)
    first, last = (max(0, -steps), min(count, count - steps))
    return lax.ppermute(value, axis, [(source, source + steps) for source in range(first, last)])


def swapped(value, axis, mask):
    return lax.ppermute(value, axis, [(i, i ^ mask) for i in range(lax.axis_size(axis))])


def place_bits(axis):
    index, bits, mask = lax.axis_index(axis), [], 1
    while mask < lax.axis_size(axis):
        bits.append((mask, lax.rem(index // mask, 2)))
        mask *= 2
    return bits


def halved(parts, dim, axis, mask, bit):
    kept = lax.dynamic_index_in_dim(parts, bit, dim, keepdims=False)
    sent = lax.dynamic_index_in_dim(parts, 1 - bit, dim, keepdims=False)
    got = swapped(sent, axis, mask)
    return (kept.astype(jnp.float32) + got.astype(jnp.float32)).astype(jnp.bfloat16)


def padded_rows(parts):
    padding = -parts.shape[1] % (8 * lax.axis_size("seq"))
    return jnp.pad(parts, ((0, 0), (0, padding), (0, 0))) if padding else parts


def summed_shards(parts, bits):
    for mask, bit in bits:
        shards, rows, columns = parts.shape
        parts = halved(parts.reshape(shards // 2, 2, rows, columns), 1, "fsdp", mask, bit)
    return parts


def summed_rows(share):
    bits = place_bits("seq")
    for mask, bit in bits:
        rows, columns = share.shape
        share = halved(share.reshape(2, rows // 2, columns), 0, "seq", mask, bit)
    for mask, bit in reversed(bits):
        other = swapped(share, "seq", mask)
        share = jnp.where(
            bit == 0, jnp.concatenate([share, other], 0), jnp.concatenate([other, share], 0)
        )
    return share


def body(tokens, cotangent, starts, w_qkv, w_attn, w_in, w_out, gain_one, gain_two):
    tok_count, model_width = tokens.shape[1:]
    head_size = model_width // HEADS
    before = passed_along(tokens[0, tok_count - HALF :], "seq", 1)
    after = passed_along(tokens[0, :HALF], "seq", -1)
    gains = lax.all_gather(jnp.stack([gain_one, gain_two]), "fsdp", axis=1, tiled=True)
    full_qkv, full_attn, full_in, full_out = (
        lax.all_gather(w_qkv, "fsdp", axis=0, tiled=True),
        lax.all_gather(w_attn, "fsdp", axis=0, tiled=True),
        lax.all_gather(w_in, "fsdp", axis=0, tiled=True),
        lax.all_gather(w_out, "fsdp", axis=0, tiled=True),
    )
    first_gain = gains[0].astype(jnp.float32)
    second_gain = gains[1].astype(jnp.float32)
    extended = jnp.concatenate([before, tokens[0], after], 0).astype(jnp.float32)
    inputs = tokens[0].astype(jnp.float32)
    ff_width = full_out.shape[0]
    seq_index = lax.axis_index("seq")
    group_length = tok_count * lax.axis_size("seq")
    seq_starts = starts[0]
    places = seq_index * tok_count - HALF + jnp.arange(tok_count + 2 * HALF, dtype=jnp.int32)
    earlier = seq_starts[None, :] <= places[:, None]
    first_token = jnp.max(jnp.where(earlier, seq_starts[None, :], 0), 1)
    position = (places - first_token).astype(jnp.float32)
    freqs = THETA ** (-jnp.arange(head_size // 2, dtype=jnp.float32) * 2.0 / head_size)
    angles = position[:, None] * freqs[None, :]
    cosine = jnp.tile(jnp.cos(angles), (1, LANES // (head_size // 2)))
    sine = jnp.tile(jnp.sin(angles), (1, LANES // (head_size // 2)))
    bounds = jnp.concatenate(
        [
            seq_starts,
            jnp.stack([seq_index * tok_count, jnp.int32(group_length)]).astype(jnp.int32),
        ]
    )
    normed_ext = norm_parts(extended, first_gain)[2].astype(jnp.bfloat16)
    mixed = jnp.dot(normed_ext, full_qkv, preferred_element_type=jnp.float32)
    query, key, value, context, probs = attend(bounds, mixed, cosine, sine, tok_count)
    hidden = inputs + jnp.dot(context, full_attn, preferred_element_type=jnp.float32)
    plain_two, spread_two, normed_two = norm_parts(hidden, second_gain)
    normed_two_low = normed_two.astype(jnp.bfloat16)
    both = jnp.dot(normed_two_low, full_in, preferred_element_type=jnp.float32)
    gate = both[:, :ff_width]
    upper = both[:, ff_width:]
    active, gelu_back = jax.vjp(lambda entry: jax.nn.gelu(entry, approximate=False), gate)
    act_low = (active * upper).astype(jnp.bfloat16)
    output = hidden + jnp.dot(act_low, full_out, preferred_element_type=jnp.float32)
    grad_result = cotangent[0]
    grad_wout = inner_product(act_low, grad_result)
    grad_act = outer_product(grad_result, full_out)
    grad_gate = gelu_back(grad_act * upper)[0]
    grad_both = jnp.concatenate([grad_gate, grad_act * active], 1).astype(jnp.bfloat16)
    grad_win = inner_product(normed_two_low, grad_both)
    grad_normed_two = outer_product(grad_both, full_in)
    grad_hidden_norm, grad_second = norm_back(grad_normed_two, plain_two, spread_two, second_gain)
    grad_hidden = grad_result.astype(jnp.float32) + grad_hidden_norm
    grad_hidden_low = grad_hidden.astype(jnp.bfloat16)
    grad_wattn = inner_product(context, grad_hidden_low)
    grad_context = outer_product(grad_hidden_low, full_attn).astype(jnp.bfloat16)

    shards = lax.axis_size("fsdp")

    def by_shard(grads):
        return grads.astype(jnp.bfloat16).reshape(shards, grads.shape[0] // shards, grads.shape[1])

    win_parts = by_shard(grad_win)
    early_parts = [
        win_parts[..., begin : begin + model_width]
        for begin in range(0, win_parts.shape[2], model_width)
    ] + [by_shard(grad_wattn), by_shard(grad_wout)]
    bits = place_bits("fsdp")
    early = summed_shards(padded_rows(jnp.concatenate(early_parts, 1)), bits[:1])
    early, grad_context = lax.optimization_barrier((early, grad_context))
    early = summed_shards(early, bits[1:])
    grad_mixed, grad_edges = attend_back(query, key, value, probs, grad_context, cosine, sine)
    from_lower = passed_along(grad_edges[HALF:], "seq", 1)
    from_upper = passed_along(grad_edges[:HALF], "seq", -1)
    grad_mixed = grad_mixed.at[:HALF, model_width:].add(from_lower)
    grad_mixed = grad_mixed.at[tok_count - HALF :, model_width:].add(from_upper)
    early, grad_mixed = lax.optimization_barrier((early, grad_mixed))
    early = summed_rows(early[0]).astype(jnp.float32)
    early_sums, begin = [], 0
    for piece in early_parts:
        early_sums.append(early[begin : begin + piece.shape[1]])
        begin += piece.shape[1]
    normed_low = normed_ext[HALF : HALF + tok_count]
    plain_one, spread_one, _ = norm_parts(inputs, first_gain)
    grad_wqkv = inner_product(normed_low, grad_mixed)
    late = summed_rows(summed_shards(padded_rows(by_shard(grad_wqkv)), bits)[0])
    grad_normed_one = outer_product(grad_mixed, full_qkv)
    grad_input_norm, grad_first = norm_back(grad_normed_one, plain_one, spread_one, first_gain)
    grad_inputs = (grad_hidden + grad_input_norm).astype(jnp.bfloat16)
    sums = jnp.stack([grad_first, grad_second]).reshape(2, shards, -1).transpose(1, 0, 2)
    for mask, bit in bits:
        halves = sums.reshape(sums.shape[0] // 2, 2, 2, sums.shape[2])
        kept = lax.dynamic_index_in_dim(halves, bit, 1, keepdims=False)
        sent = lax.dynamic_index_in_dim(halves, 1 - bit, 1, keepdims=False)
        sums = kept + swapped(sent, "fsdp", mask)
    own_gains = sums[0]
    for mask, _ in place_bits("seq"):
        own_gains = own_gains + swapped(own_gains, "seq", mask)
    return (
        output.astype(jnp.bfloat16)[None],
        grad_inputs[None],
        late[: w_qkv.shape[0]].astype(jnp.float32),
        early_sums[-2],
        jnp.concatenate(early_sums[:-2], 1),
        early_sums[-1],
        own_gains[0],
        own_gains[1],
    )


def solution(mesh):
    in_specs = (
        P("fsdp", "seq", None),
        P("fsdp", "seq", None),
        P("fsdp", None),
        P("fsdp", None),
        P("fsdp", None),
        P("fsdp", None),
        P("fsdp", None),
        P("fsdp"),
        P("fsdp"),
    )
    out_specs = (
        P("fsdp", "seq", None),
        P("fsdp", "seq", None),
        P("fsdp", None),
        P("fsdp", None),
        P("fsdp", None),
        P("fsdp", None),
        P("fsdp"),
        P("fsdp"),
    )
    return jax.shard_map(body, mesh=mesh, in_specs=in_specs, out_specs=out_specs, check_vma=False)
```
